32 devices in a mesh: space: 8 (over z, y), chan: 4 (over x, core).
Axes of the slice: x: 2, y: 2, z: 4, core: 2. Of those that a mesh axis runs over, the one named last changes fastest.
Arguments:
- latents: bfloat16 [64, 2, 640, 128], P('space', None, 'chan'), as said below
- targets: bfloat16 [64, 2, 640, 128], P('space', None, 'chan'), may hold values from -6 to 6
- norm_gain: float32 [640], P('chan'), may hold values from 0.5 to 2
- norm_bias: float32 [640], P('chan'), may hold values from -2.5 to 2.5
- conv_weight: bfloat16 [3, 3, 640, 640], P(None, None, 'chan'), may hold values from -0.078125 to 0.078125
- tile_image: int32 [8, 8], replicated, may hold values from -1 to 15, as said below
- tile_owner: int32 [8, 8], replicated, may hold values from -1 to 7, as said below
- tile_slot: int32 [8, 8], replicated, may hold values from -1 to 3, as said below
- timesteps: int32 [16], replicated, may hold values from 0 to 999
Outputs:
- x_grad: bfloat16 [32, 2, 640, 128], P('space', None, 'chan')
- weight_grad: float32 [3, 3, 640, 640], P(None, None, 'chan')
The draws below stay inside these ranges and needn't reach their ends.
Inputs may be any that keep to these rules, and one draw needn't show every extreme that they name: `tile_image`: every index s of space holds the tiles of exactly two images, each in consecutive slots in row order from the image's first row; unused slots come last and hold -1. Every image has one tile or more, all indices together hold 32 tiles, and some index has all 8 slots used. `tile_owner`: for a used slot, the index along space that computes the tile; -1 for unused slots. Every index receives exactly 4 tiles, and no index sends more than 1 tile to one index, a bound that some pair reaches. `tile_slot`: for a used slot, the tile's position among the 4 tiles of its assigned index, each position taken once; -1 for unused slots. `latents`: latent features of the images.
All inputs are finite; a program needn't handle non-finite values.
Results may differ from the reference program's by a relative error of at most 0.018.
Values may be sent and summed in bfloat16 or wider, within the bound.
A program may use at most 128 MiB of HBM per device.

```python
import math
import jax
import jax.numpy as jnp
from jax import lax

C = 640
GROUPS = 32
W = 128
TILE_ROWS = 2
TILES_DEV = 4
STORE_DEV = 8
IMAGES = 16
TILES = 32
SLOTS = 64
N_SPACE = 8


def tile_layout(key):
    base_key = jax.random.fold_in(key, 31)
    key_order, key_moved, key_split, key_dest, key_names = jax.random.split(base_key, 5)
    device_order = jax.random.permutation(key_order, N_SPACE)
    pair_count = (N_SPACE - 3) // 2
    load_shift = jnp.zeros((N_SPACE,), jnp.int32)
    load_shift = load_shift.at[0].set(TILES_DEV).at[1].set(-(TILES_DEV // 2)).at[2].set(-(TILES_DEV - TILES_DEV // 2))
    if pair_count > 0:
        moved_tiles = jax.random.randint(key_moved, (pair_count,), 0, TILES_DEV - 1).astype(jnp.int32)
        lead_index = 3 + 2 * jnp.arange(pair_count)
        load_shift = load_shift.at[lead_index].set(moved_tiles).at[lead_index + 1].set(-moved_tiles)
    load_tiles = jnp.zeros((N_SPACE,), jnp.int32).at[device_order].set(TILES_DEV + load_shift)
    first_len = jax.random.randint(key_split, (N_SPACE,), 1, load_tiles).astype(jnp.int32)
    slot_index = jnp.arange(STORE_DEV, dtype=jnp.int32)[None, :]
    occupied = slot_index < load_tiles[:, None]
    image_names = jax.random.permutation(key_names, IMAGES).astype(jnp.int32)
    local_image = 2 * jnp.arange(N_SPACE, dtype=jnp.int32)[:, None] + (slot_index >= first_len[:, None]).astype(jnp.int32)
    image_of = jnp.where(occupied, image_names[local_image], -1)
    start_tile = jnp.cumsum(load_tiles) - load_tiles
    global_tile = start_tile[:, None] + slot_index
    dest_order = jax.random.permutation(key_dest, N_SPACE).astype(jnp.int32)
    owner_of = jnp.where(occupied, dest_order[global_tile % N_SPACE], -1)
    slot_of = jnp.where(occupied, global_tile // N_SPACE, -1)
    return (image_of.astype(jnp.int32), owner_of.astype(jnp.int32), slot_of.astype(jnp.int32))


def draw_tile_image(key, part):
    return tile_layout(key)[0]


def draw_tile_owner(key, part):
    return tile_layout(key)[1]


def draw_tile_slot(key, part):
    return tile_layout(key)[2]


def draw_latents(key, part):
    sub_keys = jax.random.split(jax.random.fold_in(key, 5), 4)
    full_shape = (N_SPACE * STORE_DEV, TILE_ROWS, C, W)
    base_noise = jnp.clip(jax.random.normal(sub_keys[0], full_shape, jnp.float32), -5.0, 5.0)
    row_scale = jnp.exp(jax.random.uniform(sub_keys[1], (full_shape[0], TILE_ROWS, 1, 1), jnp.float32, 0.0, math.log(10.0)))
    chan_scale = jnp.exp(jax.random.uniform(sub_keys[2], (1, 1, C, 1), jnp.float32, 0.0, math.log(10.0)))
    offset = 0.5 * jnp.clip(jax.random.normal(sub_keys[3], (full_shape[0], 1, C, 1), jnp.float32), -4.0, 4.0)
    rise_factor = 1.0 + 2.0 * jnp.arange(full_shape[0], dtype=jnp.float32)[:, None, None, None] / (full_shape[0] - 1)
    return ((base_noise * row_scale + offset) * chan_scale * rise_factor).astype(jnp.bfloat16)


def plant(array, stream_key, least, top_value):
    extent = array.shape
    place = [jax.random.randint(jax.random.fold_in(stream_key, axis), (), 0, extent[axis]) for axis in range(len(extent))]
    array = array.at[tuple(place)].set(least)
    longest = extent.index(max(extent))
    place[longest] = (place[longest] + 1) % extent[longest]
    return array.at[tuple(place)].set(top_value)


def block_scale(key, extent, shards, least, high):
    level, own = 1.0, jax.random.fold_in(key, 6)
    for axis_at, parts in shards:
        heights = jnp.exp(jax.random.uniform(jax.random.fold_in(own, axis_at), (parts,), jnp.float32, least / len(shards), high / len(shards)))
        level = level * jnp.repeat(heights, extent[axis_at] // parts).reshape([-1 if axis == axis_at else 1 for axis in range(len(extent))])
    return level


def normal_values(own_key, dims, width, bound, pieces=(), kind=jnp.bfloat16):
    values = jax.random.normal(own_key, dims, jnp.float32) * width
    if len(pieces) > 0:
        values = block_scale(own_key, dims, pieces, -0.22, 0.18) * values
    return jnp.clip(values, min=-bound, max=bound).astype(kind)


def setup_inputs(seed: int = 0) -> dict:
    key_list = jax.random.split(jax.random.key(seed), 10)
    return {
        "latents": draw_latents(jax.random.fold_in(key_list[9], 71), 0),
        "targets": normal_values(key_list[1], (SLOTS, TILE_ROWS, C, W), 1.0, 6.0, ((0, 8), (2, 4))),
        "norm_gain": jnp.clip(0.5 + 1.5 * jax.random.uniform(key_list[2], (C,), jnp.float32) ** block_scale(key_list[2], (C,), ((0, 4),), -0.2, 0.2), 0.5, 2.0),
        "norm_bias": normal_values(key_list[3], (C,), 0.5, 2.5, ((0, 4),), jnp.float32),
        "conv_weight": normal_values(key_list[4], (3, 3, C, C), (9 * C) ** -0.5, 0.078125, ((2, 4),)),
        "tile_image": draw_tile_image(jax.random.fold_in(key_list[9], 71), 0),
        "tile_owner": draw_tile_owner(jax.random.fold_in(key_list[9], 71), 0),
        "tile_slot": draw_tile_slot(jax.random.fold_in(key_list[9], 71), 0),
        "timesteps": plant(jax.random.randint(key_list[8], (IMAGES,), 0, 1000), jax.random.fold_in(key_list[8], 1), 0, 999).astype(jnp.int32),
    }


EPS = 1e-05
HIGH = lax.Precision.HIGHEST

def loss_weights(timesteps):
    phase = (timesteps.astype(jnp.float32) / 1000.0 + 0.008) / 1.008 * (math.pi / 2.0)
    alpha_bar = jnp.cos(phase) ** 2
    return jnp.minimum(1.0, 5.0 * (1.0 - alpha_bar) / alpha_bar)

def silu_slope(pre_act):
    sigma_val = jax.nn.sigmoid(pre_act)
    return sigma_val * (1.0 + pre_act * (1.0 - sigma_val))

def group_sums(values, groups):
    grouped = values.reshape(values.shape[:-2] + (groups, values.shape[-2] // groups, values.shape[-1]))
    return lax.optimization_barrier(jnp.sum(grouped, axis=(-2, -1)))

def norm_stats(sum_first, sum_second, counts):
    mean_img = sum_first / counts[:, None]
    var_img = sum_second / counts[:, None] - mean_img * mean_img
    return (mean_img, lax.rsqrt(var_img + EPS))

def conv_views(row_views, weight):
    running = None
    for row_tap in range(3):
        source = row_views[row_tap]
        col_count = source.shape[-1]
        padded = jnp.pad(source, ((0, 0), (0, 0), (0, 0), (1, 1)))
        for col_tap in range(3):
            window = padded[:, :, :, col_tap:col_tap + col_count].astype(jnp.float32)
            tap_term = jnp.einsum('nrcw,oc->nrow', window, weight[row_tap, col_tap].astype(jnp.float32), precision=HIGH)
            running = tap_term if running is None else running + tap_term
    return running

def weight_terms(row_views, grad_field):
    grads_float = grad_field.astype(jnp.float32)
    tap_rows = []
    for row_tap in range(3):
        source = row_views[row_tap]
        col_count = source.shape[-1]
        padded = jnp.pad(source, ((0, 0), (0, 0), (0, 0), (1, 1)))
        tap_cols = []
        for col_tap in range(3):
            window = padded[:, :, :, col_tap:col_tap + col_count].astype(jnp.float32)
            tap_cols.append(jnp.einsum('nrow,nrcw->oc', grads_float, window, precision=HIGH))
        tap_rows.append(jnp.stack(tap_cols))
    return jnp.stack(tap_rows)

def shifted_views(source_field, up_ok, down_ok):
    zero_rows = jnp.zeros_like(source_field[:, :1])
    up_mask = up_ok.astype(source_field.dtype)[None, :, None, None]
    down_mask = down_ok.astype(source_field.dtype)[None, :, None, None]
    rows_above = jnp.concatenate([zero_rows, source_field[:, :-1]], axis=1) * up_mask
    rows_below = jnp.concatenate([source_field[:, 1:], zero_rows], axis=1) * down_mask
    return [rows_above, source_field, rows_below]

def device_pass(lat_dev, tar_dev, image_dev, norm_gain, norm_bias, conv_weight, flipped, counts, weights_img):
    row_total = STORE_DEV * TILE_ROWS
    group_size = C // GROUPS
    row_image = jnp.repeat(image_dev, TILE_ROWS)
    row_valid = row_image >= 0
    prev_image = jnp.concatenate([jnp.full((1,), -2, jnp.int32), row_image[:-1]])
    next_image = jnp.concatenate([row_image[1:], jnp.full((1,), -2, jnp.int32)])
    up_ok = row_valid & (prev_image == row_image)
    down_ok = row_valid & (next_image == row_image)
    image_ids = jnp.arange(IMAGES, dtype=jnp.int32)
    onehot = (row_image[:, None] == image_ids[None, :]).astype(jnp.float32)
    lat_float = lat_dev.reshape(1, row_total, C, W).astype(jnp.float32)
    part_first = jnp.dot(onehot.T, group_sums(lat_float, GROUPS)[0], precision=HIGH)
    part_second = jnp.dot(onehot.T, group_sums(lat_float * lat_float, GROUPS)[0], precision=HIGH)
    mean_img, rstd_img = norm_stats(part_first, part_second, counts)
    mean_rows = jnp.repeat(jnp.dot(onehot, mean_img, precision=HIGH), group_size, axis=1)[None, :, :, None]
    rstd_rows = jnp.repeat(jnp.dot(onehot, rstd_img, precision=HIGH), group_size, axis=1)[None, :, :, None]
    valid_rows = row_valid.astype(jnp.float32)[None, :, None, None]
    normed = (lat_float - mean_rows) * rstd_rows
    pre_act = normed * norm_gain[:, None] + norm_bias[:, None]
    act = (jax.nn.silu(pre_act) * valid_rows).astype(jnp.bfloat16)
    prediction = conv_views(shifted_views(act, up_ok, down_ok), conv_weight)
    loss_rows = jnp.dot(onehot, weights_img, precision=HIGH)[None, :, None, None]
    target_float = tar_dev.reshape(1, row_total, C, W).astype(jnp.float32)
    out_grad = (loss_rows * (prediction - target_float) * valid_rows).astype(jnp.bfloat16)
    act_grad = conv_views(shifted_views(out_grad, up_ok, down_ok), flipped)
    norm_grad = act_grad * silu_slope(pre_act) * norm_gain[:, None]
    grad_first = jnp.dot(onehot.T, group_sums(norm_grad, GROUPS)[0], precision=HIGH)
    grad_second = jnp.dot(onehot.T, group_sums(norm_grad * normed, GROUPS)[0], precision=HIGH)
    mean_g = jnp.repeat(jnp.dot(onehot, grad_first / counts[:, None], precision=HIGH), group_size, axis=1)[None, :, :, None]
    mean_gn = jnp.repeat(jnp.dot(onehot, grad_second / counts[:, None], precision=HIGH), group_size, axis=1)[None, :, :, None]
    x_grad = (rstd_rows * (norm_grad - mean_g - normed * mean_gn) * valid_rows).astype(jnp.bfloat16)
    weight_sum = weight_terms(shifted_views(act, up_ok, down_ok), out_grad)
    return (x_grad.reshape(STORE_DEV, TILE_ROWS, C, W), weight_sum)

def reference(latents, targets, norm_gain, norm_bias, conv_weight, tile_image, tile_owner, tile_slot, timesteps):
    group_size = C // GROUPS
    image_ids = jnp.arange(IMAGES, dtype=jnp.int32)
    counts = lax.optimization_barrier(jnp.sum((tile_image.reshape(-1)[None, :] == image_ids[:, None]).astype(jnp.float32), axis=1)) * float(TILE_ROWS * W * group_size)
    weights_img = loss_weights(timesteps)
    flipped = jnp.transpose(conv_weight[::-1, ::-1], (0, 1, 3, 2))
    lat_split = latents.reshape(N_SPACE, STORE_DEV, TILE_ROWS, C, W)
    tar_split = targets.reshape(N_SPACE, STORE_DEV, TILE_ROWS, C, W)

    def one_device(carry, device_inputs):
        grad_tiles, weight_sum = device_pass(device_inputs[0], device_inputs[1], device_inputs[2], norm_gain, norm_bias, conv_weight, flipped, counts, weights_img)
        return (carry + weight_sum, grad_tiles)
    weight_total, grad_tiles = lax.scan(one_device, jnp.zeros((3, 3, C, C), jnp.float32), (lat_split, tar_split, tile_image))
    dest_index = jnp.where(tile_owner >= 0, tile_owner * TILES_DEV + tile_slot, TILES).reshape(-1).astype(jnp.int32)
    x_grad = jnp.zeros((TILES, TILE_ROWS, C, W), jnp.bfloat16).at[dest_index].set(grad_tiles.reshape(SLOTS, TILE_ROWS, C, W), mode='drop')
    weight_grad = weight_total / math.sqrt(TILES * TILE_ROWS * W)
    return (x_grad, weight_grad)
```

```python
import math

import jax
import jax.numpy as jnp
from jax import lax
from jax.sharding import PartitionSpec as P

GROUPS = 32


EPS = 1e-05
HIGH = lax.Precision.HIGHEST


def loss_weights(timesteps):
    phase = (timesteps.astype(jnp.float32) / 1000.0 + 0.008) / 1.008 * (math.pi / 2.0)
    alpha_bar = jnp.cos(phase) ** 2
    return jnp.minimum(1.0, 5.0 * (1.0 - alpha_bar) / alpha_bar)


def silu_slope(pre_act):
    sigma_val = jax.nn.sigmoid(pre_act)
    return sigma_val * (1.0 + pre_act * (1.0 - sigma_val))


def group_sums(values, groups):
    grouped = values.reshape(
        values.shape[:-2] + (groups, values.shape[-2] // groups, values.shape[-1])
    )
    return jnp.sum(grouped, axis=(-2, -1))


def norm_stats(sum_first, sum_second, counts):
    mean_img = sum_first / counts[:, None]
    var_img = sum_second / counts[:, None] - mean_img * mean_img
    return (mean_img, lax.rsqrt(var_img + EPS))


def conv_views(row_views, weight):
    running = None
    for row_tap in range(3):
        source = row_views[row_tap]
        col_count = source.shape[-1]
        padded = jnp.pad(source, ((0, 0), (0, 0), (0, 0), (1, 1)))
        for col_tap in range(3):
            window = padded[:, :, :, col_tap : col_tap + col_count]
            tap_term = jnp.einsum(
                "nrcw,oc->nrow",
                window,
                weight[row_tap, col_tap],
                preferred_element_type=jnp.float32,
            )
            running = tap_term if running is None else running + tap_term
    return running


def weight_terms(row_views, grad_field):
    tap_rows = []
    for row_tap in range(3):
        source = row_views[row_tap]
        col_count = source.shape[-1]
        padded = jnp.pad(source, ((0, 0), (0, 0), (0, 0), (1, 1)))
        tap_cols = []
        for col_tap in range(3):
            window = padded[:, :, :, col_tap : col_tap + col_count]
            tap_cols.append(
                jnp.einsum("nrow,nrcw->oc", grad_field, window, preferred_element_type=jnp.float32)
            )
        tap_rows.append(jnp.stack(tap_cols))
    return jnp.stack(tap_rows)


def gather_channels(act):
    return lax.all_gather(act, "chan", axis=2, tiled=True)


def sum_channels(partial_grad):
    return lax.psum_scatter(
        partial_grad.astype(jnp.bfloat16), "chan", scatter_dimension=2, tiled=True
    ).astype(jnp.float32)


def receive_tiles(outgoing):
    return lax.all_to_all(outgoing, "space", split_axis=0, concat_axis=0, tiled=True)


def local(
    latents,
    targets,
    norm_gain,
    norm_bias,
    conv_weight,
    tile_image,
    tile_owner,
    tile_slot,
    timesteps,
):
    my_index = lax.axis_index("space")
    devices = lax.axis_size("space")
    slots_dev, tile_rows, local_ch, col_count = latents.shape
    channels = conv_weight.shape[3]
    group_size = channels // GROUPS
    groups_here = local_ch // group_size
    image_total = timesteps.shape[0]
    tiles_dev = slots_dev // 2
    image_ids = jnp.arange(image_total, dtype=jnp.int32)
    counts = jnp.sum(
        (tile_image.reshape(-1)[None, :] == image_ids[:, None]).astype(jnp.float32), axis=1
    ) * float(tile_rows * col_count * group_size)
    weights_img = loss_weights(timesteps)
    flipped = jnp.transpose(conv_weight[::-1, ::-1], (0, 1, 3, 2))
    gain_col = norm_gain[:, None]
    bias_col = norm_bias[:, None]
    grad_scale = 1.0 / math.sqrt(devices * tiles_dev * tile_rows * col_count)
    my_image = lax.dynamic_index_in_dim(tile_image, my_index, 0, keepdims=False)
    my_owner = lax.dynamic_index_in_dim(tile_owner, my_index, 0, keepdims=False)
    rows = slots_dev * tile_rows
    row_image = jnp.repeat(my_image, tile_rows)
    valid = row_image >= 0
    edge = jnp.full((1,), -2, jnp.int32)
    up_ok = valid & (jnp.concatenate([edge, row_image[:-1]]) == row_image)
    down_ok = valid & (jnp.concatenate([row_image[1:], edge]) == row_image)
    onehot = (row_image[:, None] == image_ids[None, :]).astype(jnp.float32)

    def shifted(field):
        zero = jnp.zeros_like(field[:, :1])
        above = jnp.concatenate([zero, field[:, :-1]], axis=1)
        below = jnp.concatenate([field[:, 1:], zero], axis=1)
        above = jnp.where(up_ok[None, :, None, None], above, 0)
        below = jnp.where(down_ok[None, :, None, None], below, 0)
        return [above, field, below]

    def per_row(per_image):
        out = jnp.dot(onehot, per_image, precision=HIGH)
        return jnp.repeat(out, group_size, axis=1)[None, :, :, None]

    def per_image(values):
        return jnp.dot(onehot.T, group_sums(values, groups_here)[0], precision=HIGH)

    lat = latents.reshape(1, rows, local_ch, col_count).astype(jnp.float32)
    mean_img, rstd_img = norm_stats(
        per_image(lat), per_image(lat * lat), jnp.maximum(counts, 1.0)
    )
    mean_rows, rstd_rows = per_row(mean_img), per_row(rstd_img)
    valid_rows = valid[None, :, None, None]
    normed = (lat - mean_rows) * rstd_rows
    pre_act = normed * gain_col + bias_col
    act = jnp.where(valid_rows, jax.nn.silu(pre_act), 0.0).astype(jnp.bfloat16)
    views = shifted(gather_channels(act))
    prediction = conv_views(views, conv_weight)
    loss_rows = jnp.dot(onehot, weights_img, precision=HIGH)[None, :, None, None]
    target = targets.reshape(1, rows, local_ch, col_count).astype(jnp.float32)
    out_grad = jnp.where(valid_rows, loss_rows * (prediction - target), 0.0).astype(jnp.bfloat16)
    weight_sum = weight_terms(views, out_grad)
    weight_grad = lax.psum((weight_sum * grad_scale).astype(jnp.bfloat16), "space").astype(
        jnp.float32
    )
    act_grad = sum_channels(conv_views(shifted(out_grad), flipped))
    norm_grad = act_grad * silu_slope(pre_act) * gain_col
    mean_g = per_row(per_image(norm_grad) / jnp.maximum(counts, 1.0)[:, None])
    mean_gn = per_row(per_image(norm_grad * normed) / jnp.maximum(counts, 1.0)[:, None])
    x_grad = (rstd_rows * (norm_grad - mean_g - normed * mean_gn)).astype(jnp.bfloat16)
    x_tiles = x_grad.reshape(latents.shape)
    device_ids = jnp.arange(devices, dtype=jnp.int32)
    from_slot = jnp.argmax(my_owner[None, :] == device_ids[:, None], axis=1)
    outgoing = jnp.stack(
        [lax.dynamic_index_in_dim(x_tiles, from_slot[d], 0, False) for d in range(devices)]
    )
    arrived = receive_tiles(outgoing)
    slot_ids = jnp.arange(tiles_dev, dtype=jnp.int32)
    hits = (tile_owner[None] == my_index) & (tile_slot[None] == slot_ids[:, None, None])
    source = jnp.argmax(jnp.any(hits, axis=2), axis=1)
    x_out = jnp.stack(
        [lax.dynamic_index_in_dim(arrived, source[t], 0, False) for t in range(tiles_dev)]
    )
    return (x_out, weight_grad)


def solution(mesh):
    in_specs = (
        P("space", None, "chan", None),
        P("space", None, "chan", None),
        P("chan"),
        P("chan"),
        P(None, None, "chan", None),
        P(),
        P(),
        P(),
        P(),
    )
    out_specs = (P("space", None, "chan", None), P(None, None, "chan", None))
    return jax.shard_map(local, mesh=mesh, in_specs=in_specs, out_specs=out_specs, check_vma=False)
```

```python
import functools
import math

import jax
import jax.numpy as jnp
from jax import lax
from jax.experimental import pallas as pl
from jax.experimental.pallas import tpu as pltpu
from jax.sharding import PartitionSpec as P

GROUPS = 32
EPS = 1e-05
HIGH = lax.Precision.HIGHEST
F32, BF16 = jnp.float32, jnp.bfloat16
MESH = pl.DeviceIdType.MESH
CHUNKS = 4


def loss_weights(timesteps):
    phase = (timesteps.astype(F32) / 1000.0 + 0.008) / 1.008 * (math.pi / 2.0)
    alpha_bar = jnp.cos(phase) ** 2
    return jnp.minimum(1.0, 5.0 * (1.0 - alpha_bar) / alpha_bar)


def kernel(
    n, grad_scale, ti, to, ts, lw, gb, lat, tgt, w, xo, wo,
    act, mybuf, agbuf, act_t, pre_w, field, w_t, wbuf, wy, ybuf, zsend, zbuf, own, gzbuf, gybuf,
    part, sib_far, sib_near, x_send, x_recv, stat, ngrad, xg, outg, inb,
    ag_send, ag_recv, y_send, y_recv, z_send, z_recv, gz_send, gz_recv,
    gy_send, gy_recv, a_send, a_recv, r_send, r_recv,
):
    slots, trows, loc, cols = lat.shape
    nrow = slots * trows
    rows9, chans = w.shape
    tiles_dev = xo.shape[0]
    group = chans // GROUPS
    nz = n // 2
    piece = wbuf.shape[1]
    half = nz * piece
    padded = 2 * half
    span = nrow * cols // CHUNKS
    me = lax.axis_index("space")
    ch = lax.axis_index("chan")
    my_y, my_z = lax.rem(me, 2), me // 2
    y_dev = my_z * 2 + 1 - my_y
    core, my_x = lax.rem(ch, 2), ch // 2
    sib = my_x * 2 + 1 - core
    xn = (1 - my_x) * 2 + core
    diag = (1 - my_x) * 2 + 1 - core

    def rc(src, dst, ss, rs, space=None, chan=None):
        return pltpu.make_async_remote_copy(
            src_ref=src, dst_ref=dst, send_sem=ss, recv_sem=rs,
            device_id={
                "space": me if space is None else space,
                "chan": ch if chan is None else chan,
            },
            device_id_type=MESH,
        )

    barrier = pltpu.get_barrier_semaphore()
    for k in range(1, n):
        pl.semaphore_signal(
            barrier, inc=1, device_id={"space": lax.rem(me + k, n), "chan": ch},
            device_id_type=MESH,
        )
    for other in (sib, xn):
        pl.semaphore_signal(
            barrier, inc=1, device_id={"space": me, "chan": other}, device_id_type=MESH
        )

    image = [ti[me, j] for j in range(slots)]
    first = image[0]
    used_i = [(v >= 0).astype(jnp.int32) for v in image]
    is_b = [jnp.where((v >= 0) & (v != first), 1, 0) for v in image]
    used = [u.astype(F32) for u in used_i]
    mask_b = [b.astype(F32) for b in is_b]
    mask_a = [u - b for u, b in zip(used, mask_b)]
    same = [
        jnp.where((image[j] >= 0) & (image[j] == image[j + 1]), 1.0, 0.0).astype(F32)
        for j in range(slots - 1)
    ]
    per_slot = float(trows * cols * group)
    count_a = jnp.maximum(sum(mask_a), 1.0) * per_slot
    count_b = jnp.maximum(sum(mask_b), 1.0) * per_slot
    loss = [lw[jnp.maximum(v, 0)] * u for v, u in zip(image, used)]
    up = [(1.0 if r % trows else (same[r // trows - 1] if r else 0.0)) for r in range(nrow)]
    up = [u * used[r // trows] for r, u in enumerate(up)]
    down = [
        (1.0 if r % trows < trows - 1 else (same[r // trows] if r < nrow - 1 else 0.0))
        for r in range(nrow)
    ]
    down = [u * used[r // trows] for r, u in enumerate(down)]

    gain, bias = gb[0], gb[1]
    chan_row = lax.broadcasted_iota(jnp.int32, (loc, loc), 0) // group
    chan_col = lax.broadcasted_iota(jnp.int32, (loc, loc), 1) // group
    same_group = jnp.where(chan_row == chan_col, 1.0, 0.0).astype(F32)
    lane = lax.broadcasted_iota(jnp.int32, (loc, cols), 1)

    def group_total(values):
        summed = jnp.sum(values, axis=1, keepdims=True)
        wide = jnp.broadcast_to(summed, (loc, cols))
        return jnp.dot(same_group, wide, precision=HIGH, preferred_element_type=F32)

    sums = [jnp.zeros((loc, cols), F32) for _ in range(4)]
    for j in range(slots):
        x0 = lat[j, 0].astype(F32)
        total, square = x0, x0 * x0
        for t in range(1, trows):
            xt = lat[j, t].astype(F32)
            total, square = total + xt, square + xt * xt
        sums = [
            sums[0] + mask_a[j] * total, sums[1] + mask_a[j] * square,
            sums[2] + mask_b[j] * total, sums[3] + mask_b[j] * square,
        ]
    for i, count in enumerate((count_a, count_b)):
        mean = group_total(sums[2 * i]) / count
        var = group_total(sums[2 * i + 1]) / count - mean * mean
        stat[i, 0] = mean
        stat[i, 1] = lax.rsqrt(var + EPS)

    def pre_of(r):
        j = r // trows
        mean, rstd = stat[is_b[j], 0], stat[is_b[j], 1]
        normed = (lat[j, r % trows].astype(F32) - mean) * rstd
        return normed, normed * gain + bias, rstd

    mine = pl.ds(pl.multiple_of(ch * loc, 16), loc)

    def ag_copy(kind, c):
        source = (mybuf.at[c], mybuf.at[c], agbuf.at[1, c])[kind]
        return rc(
            source, agbuf.at[kind, c], ag_send.at[kind, c], ag_recv.at[kind, c],
            chan=(sib, xn, sib)[kind],
        )

    pl.semaphore_wait(barrier, n + 1)
    for c in range(CHUNKS):
        for r in range(c * nrow // CHUNKS, (c + 1) * nrow // CHUNKS):
            _, pre, _ = pre_of(r)
            value = pre * jax.nn.sigmoid(pre) * used[r // trows]
            mybuf[c, :, pl.ds(r * cols - c * span, cols)] = value.astype(BF16)
        ag_copy(1, c).start()
        ag_copy(0, c).start()

    pad = padded - rows9
    full_blocks = rows9 // 128
    for i in range(full_blocks):
        w_t[:, pl.ds(i * 128, 128)] = w[pl.ds(i * 128, 128), :].T
    rest = rows9 - full_blocks * 128
    if rest:
        tail = jnp.concatenate(
            [w[pl.ds(full_blocks * 128, rest), :], jnp.zeros((128 - rest, chans), BF16)], axis=0
        )
        w_t[:, pl.ds(full_blocks * 128, 128)] = tail.T
        done = (full_blocks + 1) * 128
    else:
        done = rows9
    if done < rows9 + pad:
        w_t[:, pl.ds(done, rows9 + pad - done)] = jnp.zeros((chans, rows9 + pad - done), BF16)
    field[pl.ds(rows9, pad), :] = jnp.zeros((pad, nrow * cols), BF16)
    third = rows9 // 3
    field[pl.ds(0, third), pl.ds((nrow - 1) * cols, cols)] = jnp.zeros((third, cols), BF16)
    field[pl.ds(2 * third, third), pl.ds(0, cols)] = jnp.zeros((third, cols), BF16)

    def from_left(v):
        return jnp.where(lane == 0, 0.0, pltpu.roll(v, 1, 1))

    def from_right(v):
        return jnp.where(lane == cols - 1, 0.0, pltpu.roll(v, cols - 1, 1))

    def taps(row_tap, col_tap, r):
        return pre_w[pl.ds((row_tap * 3 + col_tap) * loc, loc), pl.ds(r * cols, cols)]

    def out_row(r):
        j = r // trows
        total = []
        for col_tap in range(3):
            value = taps(1, col_tap, r)
            if r > 0:
                value = value + up[r] * taps(0, col_tap, r - 1)
            if r < nrow - 1:
                value = value + down[r] * taps(2, col_tap, r + 1)
            total.append(value)
        pred = total[1] + from_left(total[0]) + from_right(total[2])
        grad = loss[j] * (pred - tgt[j, r % trows].astype(F32))
        grad = grad.astype(BF16).astype(F32)
        for col_tap, moved in enumerate((from_right(grad), grad, from_left(grad))):
            def put(row_tap, row, value):
                field[
                    pl.ds((row_tap * 3 + col_tap) * loc, loc), pl.ds(row * cols, cols)
                ] = value.astype(BF16)
            put(1, r, moved)
            if r > 0:
                put(0, r - 1, up[r] * moved)
            if r < nrow - 1:
                put(2, r + 1, down[r] * moved)

    rows_chunk = nrow // CHUNKS
    for c in range(CHUNKS):
        ag_copy(1, c).wait_recv()
        ag_copy(2, c).start()
        ag_copy(0, c).wait_recv()
        ag_copy(2, c).wait_recv()
        here = pl.ds(c * span, span)
        act[mine, here] = mybuf[c]
        for kind, index in enumerate((sib, xn, diag)):
            act[pl.ds(pl.multiple_of(index * loc, 16), loc), here] = agbuf[kind, c]
        for i in range(3):
            pre_w[pl.ds(i * third, third), here] = jnp.dot(
                w[pl.ds(i * third, third), :], act[:, here], preferred_element_type=F32
            )
        act_t[here, :] = act[:, here].T
        low = max(0, c * rows_chunk - 1)
        high = nrow if c == CHUNKS - 1 else (c + 1) * rows_chunk - 1
        for r in range(low, high):
            out_row(r)

    def weight_part(y):
        start = pl.multiple_of(y * half, 16)
        total = jnp.dot(field[pl.ds(start, half), :], act_t[...], preferred_element_type=F32)
        return (total * grad_scale).astype(BF16).reshape(nz, piece, chans)

    def y_copy(k):
        return rc(
            wy.at[lax.rem(my_z + k, nz)], ybuf.at[k], y_send.at[k], y_recv.at[k], space=y_dev
        )

    order = list(range(1, nz)) + [0]
    wy[...] = weight_part(1 - my_y)
    for k in order:
        y_copy(k).start()
    wbuf[...] = weight_part(my_y)

    for c in range(CHUNKS):
        here = pl.ds(c * span, span)
        part[:, here] = jnp.dot(
            w_t[...], field[:, here], preferred_element_type=F32
        ).astype(BF16)

    def block(index):
        return pl.ds(pl.multiple_of(index * loc, 16), loc)

    far_copy = rc(part.at[block(diag)], sib_far, r_send.at[0], r_recv.at[0], chan=sib)
    near_copy = rc(part.at[block(sib)], sib_near, r_send.at[1], r_recv.at[1], chan=sib)
    x_copy = rc(x_send, x_recv, r_send.at[2], r_recv.at[2], chan=xn)
    far_copy.start()
    near_copy.start()
    far_copy.wait_recv()
    x_send[...] = (part[block(xn), :].astype(F32) + sib_far[...].astype(F32)).astype(BF16)
    x_copy.start()

    def z_copy(k):
        z = lax.rem(my_z + k, nz)
        return rc(
            zsend.at[k], zbuf.at[k], z_send.at[k], z_recv.at[k], space=z * 2 + my_y
        )

    for k in order:
        y_copy(k).wait_recv()
        z = lax.rem(my_z + k, nz)
        zsend[k] = (wbuf[z].astype(F32) + ybuf[k].astype(F32)).astype(BF16)
        if k:
            z_copy(k).start()

    near_copy.wait_recv()
    x_copy.wait_recv()
    sums = [jnp.zeros((loc, cols), F32) for _ in range(4)]
    for j in range(slots):
        total, second = None, None
        for t in range(trows):
            r = j * trows + t
            at = pl.ds(r * cols, cols)
            grad = (
                part[mine, at].astype(F32) + sib_near[:, at].astype(F32)
            ) + x_recv[:, at].astype(F32)
            normed, pre, _ = pre_of(r)
            s = jax.nn.sigmoid(pre)
            value = grad * (s * (1.0 + pre * (1.0 - s))) * gain
            ngrad[r] = value
            total = value if total is None else total + value
            second = value * normed if second is None else second + value * normed
        sums = [
            sums[0] + mask_a[j] * total, sums[1] + mask_a[j] * second,
            sums[2] + mask_b[j] * total, sums[3] + mask_b[j] * second,
        ]
    for i, count in enumerate((count_a, count_b)):
        stat[i, 2] = group_total(sums[2 * i]) / count
        stat[i, 3] = group_total(sums[2 * i + 1]) / count
    for r in range(nrow):
        j = r // trows
        normed, _, rstd = pre_of(r)
        mean_g, mean_gn = stat[is_b[j], 2], stat[is_b[j], 3]
        xg[j, r % trows] = (rstd * (ngrad[r] - mean_g - normed * mean_gn)).astype(BF16)
    for k in range(n):
        d = lax.rem(me + k, n)
        slot = jnp.int32(0)
        for j in range(slots):
            slot = jnp.where(to[me, j] == d, j, slot)
        if k:
            outg[k] = xg[slot]
        else:
            inb[0] = xg[slot]

    total = zsend[0].astype(F32)
    for k in range(1, nz):
        z_copy(k).wait_recv()
        total = total + zbuf[k].astype(F32)
    own[...] = total.astype(BF16)

    def gz_copy(k):
        z = lax.rem(my_z + k, nz)
        return rc(own, gzbuf.at[k], gz_send.at[k], gz_recv.at[k], space=z * 2 + my_y)

    def gy_copy(k):
        source = gzbuf.at[k] if k else own
        return rc(source, gybuf.at[k], gy_send.at[k], gy_recv.at[k], space=y_dev)

    for k in range(1, nz):
        gz_copy(k).start()
    gy_copy(0).start()

    def a_copy(k):
        return rc(
            outg.at[k], inb.at[k], a_send.at[k], a_recv.at[k], space=lax.rem(me + k, n)
        )

    for k in range(1, n):
        a_copy(k).start()

    def put_piece(y, k, value):
        z = lax.rem(my_z - k + nz, nz)
        wo[pl.ds(pl.multiple_of((y * nz + z) * piece, 16), piece), :] = value

    put_piece(my_y, 0, own[...])
    for k in range(1, nz):
        gz_copy(k).wait_recv()
        gy_copy(k).start()
        put_piece(my_y, k, gzbuf[k])

    def find(step, found):
        s, j = step // slots, lax.rem(step, slots)
        owner, place = to[s, j], ts[s, j]
        return tuple(
            jnp.where((owner == me) & (place == t), s, found[t]) for t in range(tiles_dev)
        )

    found = lax.fori_loop(0, n * slots, find, tuple(jnp.int32(0) for _ in range(tiles_dev)))
    for k in range(1, n):
        a_copy(k).wait_recv()
    for t in range(tiles_dev):
        xo[t] = inb[lax.rem(me - found[t] + n, n)]
    for k in range(nz):
        gy_copy(k).wait_recv()
        put_piece(1 - my_y, k, gybuf[k])

    for c in range(CHUNKS):
        for kind in range(3):
            ag_copy(kind, c).wait_send()
    for z in range(nz):
        y_copy(z).wait_send()
        gy_copy(z).wait_send()
    for k in range(1, nz):
        z_copy(k).wait_send()
        gz_copy(k).wait_send()
    for k in range(1, n):
        a_copy(k).wait_send()
    for copy in (far_copy, near_copy, x_copy):
        copy.wait_send()


def local(
    latents, targets, norm_gain, norm_bias, conv_weight, tile_image, tile_owner, tile_slot,
    timesteps,
):
    n = lax.axis_size("space")
    slots, trows, loc, cols = latents.shape
    chans = conv_weight.shape[3]
    tiles_dev = slots // 2
    rows9 = 9 * loc
    wide = slots * trows * cols
    step = math.lcm(16 * n, 256)
    padded = -(-rows9 // step) * step
    nz = n // 2
    piece = padded // n
    grad_scale = 1.0 / math.sqrt(n * tiles_dev * trows * cols)
    gb = jnp.broadcast_to(
        jnp.stack([norm_gain, norm_bias])[:, :, None], (2, loc, cols)
    )
    smem = pl.BlockSpec(memory_space=pltpu.SMEM)
    vmem = pl.BlockSpec(memory_space=pltpu.VMEM)
    dma = pltpu.SemaphoreType.DMA
    x_grad, weight = pl.pallas_call(
        functools.partial(kernel, n, grad_scale),
        out_shape=(
            jax.ShapeDtypeStruct((tiles_dev, trows, loc, cols), BF16),
            jax.ShapeDtypeStruct((padded, chans), BF16),
        ),
        in_specs=[smem] * 4 + [vmem] * 4,
        out_specs=(vmem, vmem),
        scratch_shapes=[
            pltpu.VMEM((chans, wide), BF16),
            pltpu.VMEM((CHUNKS, loc, wide // CHUNKS), BF16),
            pltpu.VMEM((3, CHUNKS, loc, wide // CHUNKS), BF16),
            pltpu.VMEM((wide, chans), BF16),
            pltpu.VMEM((rows9, wide), F32),
            pltpu.VMEM((padded, wide), BF16),
            pltpu.VMEM((chans, padded), BF16),
            *[pltpu.VMEM((nz, piece, chans), BF16)] * 5,
            pltpu.VMEM((piece, chans), BF16),
            *[pltpu.VMEM((nz, piece, chans), BF16)] * 2,
            pltpu.VMEM((chans, wide), BF16),
            pltpu.VMEM((loc, wide), BF16),
            pltpu.VMEM((loc, wide), BF16),
            pltpu.VMEM((loc, wide), BF16),
            pltpu.VMEM((loc, wide), BF16),
            pltpu.VMEM((2, 4, loc, cols), F32),
            pltpu.VMEM((slots * trows, loc, cols), F32),
            pltpu.VMEM((slots, trows, loc, cols), BF16),
            pltpu.VMEM((n, trows, loc, cols), BF16),
            pltpu.VMEM((n, trows, loc, cols), BF16),
            dma((3, CHUNKS)), dma((3, CHUNKS)),
            dma((nz,)), dma((nz,)), dma((nz,)), dma((nz,)), dma((nz,)), dma((nz,)),
            dma((nz,)), dma((nz,)), dma((n,)), dma((n,)), dma((3,)), dma((3,)),
        ],
        compiler_params=pltpu.CompilerParams(
            collective_id=0, has_side_effects=True, vmem_limit_bytes=62 * 1024 * 1024
        ),
    )(
        tile_image, tile_owner, tile_slot, loss_weights(timesteps), gb, latents, targets,
        conv_weight.reshape(rows9, chans),
    )
    return x_grad, weight[:rows9].astype(F32).reshape(conv_weight.shape)


def solution(mesh):
    in_specs = (
        P("space", None, "chan", None),
        P("space", None, "chan", None),
        P("chan"),
        P("chan"),
        P(None, None, "chan", None),
        P(),
        P(),
        P(),
        P(),
    )
    out_specs = (P("space", None, "chan", None), P(None, None, "chan", None))
    return jax.shard_map(local, mesh=mesh, in_specs=in_specs, out_specs=out_specs, check_vma=False)
```

```python
import functools
import math

import jax
import jax.numpy as jnp
from jax import lax
from jax.experimental import pallas as pl
from jax.experimental.pallas import tpu as pltpu
from jax.sharding import PartitionSpec as P

GROUPS = 32
EPS = 1e-05
HIGH = lax.Precision.HIGHEST
F32, BF16 = jnp.float32, jnp.bfloat16
MESH = pl.DeviceIdType.MESH
CHUNKS = 4


def loss_weights(timesteps):
    phase = (timesteps.astype(F32) / 1000.0 + 0.008) / 1.008 * (math.pi / 2.0)
    alpha_bar = jnp.cos(phase) ** 2
    return jnp.minimum(1.0, 5.0 * (1.0 - alpha_bar) / alpha_bar)


def kernel(
    n, grad_scale, ti, to, ts, lw, gb, lat, tgt, w, xo, wo,
    act, mybuf, agbuf, act_t, pre_w, field, w_t, wbuf, wy, ybuf, zsend, zbuf, own, gzbuf, gybuf, res,
    part, sib_far, sib_near, x_send, x_recv, stat, ngrad, xg, outg, inb,
    ag_send, ag_recv, y_send, y_recv, z_send, z_recv, gz_send, gz_recv,
    gy_send, gy_recv, a_send, a_recv, r_send, r_recv,
):
    slots, trows, loc, cols = lat.shape
    nrow = slots * trows
    rows9, chans = w.shape
    tiles_dev = xo.shape[0]
    group = chans // GROUPS
    nz = n // 2
    piece = wbuf.shape[1]
    half = nz * piece
    padded = 2 * half
    span = nrow * cols // CHUNKS
    me = lax.axis_index("space")
    ch = lax.axis_index("chan")
    my_y, my_z = lax.rem(me, 2), me // 2
    y_dev = my_z * 2 + 1 - my_y
    core, my_x = lax.rem(ch, 2), ch // 2
    sib = my_x * 2 + 1 - core
    xn = (1 - my_x) * 2 + core
    diag = (1 - my_x) * 2 + 1 - core

    def rc(src, dst, ss, rs, space=None, chan=None):
        return pltpu.make_async_remote_copy(
            src_ref=src, dst_ref=dst, send_sem=ss, recv_sem=rs,
            device_id={
                "space": me if space is None else space,
                "chan": ch if chan is None else chan,
            },
            device_id_type=MESH,
        )

    barrier = pltpu.get_barrier_semaphore()
    for k in range(1, n):
        pl.semaphore_signal(
            barrier, inc=1, device_id={"space": lax.rem(me + k, n), "chan": ch},
            device_id_type=MESH,
        )
    for other in (sib, xn):
        pl.semaphore_signal(
            barrier, inc=1, device_id={"space": me, "chan": other}, device_id_type=MESH
        )

    image = [ti[me, j] for j in range(slots)]
    first = image[0]
    used_i = [(v >= 0).astype(jnp.int32) for v in image]
    is_b = [jnp.where((v >= 0) & (v != first), 1, 0) for v in image]
    used = [u.astype(F32) for u in used_i]
    mask_b = [b.astype(F32) for b in is_b]
    mask_a = [u - b for u, b in zip(used, mask_b)]
    same = [
        jnp.where((image[j] >= 0) & (image[j] == image[j + 1]), 1.0, 0.0).astype(F32)
        for j in range(slots - 1)
    ]
    per_slot = float(trows * cols * group)
    count_a = jnp.maximum(sum(mask_a), 1.0) * per_slot
    count_b = jnp.maximum(sum(mask_b), 1.0) * per_slot
    loss = [lw[jnp.maximum(v, 0)] * u for v, u in zip(image, used)]
    up = [(1.0 if r % trows else (same[r // trows - 1] if r else 0.0)) for r in range(nrow)]
    up = [u * used[r // trows] for r, u in enumerate(up)]
    down = [
        (1.0 if r % trows < trows - 1 else (same[r // trows] if r < nrow - 1 else 0.0))
        for r in range(nrow)
    ]
    down = [u * used[r // trows] for r, u in enumerate(down)]

    gain, bias = gb[0], gb[1]
    chan_row = lax.broadcasted_iota(jnp.int32, (loc, loc), 0) // group
    chan_col = lax.broadcasted_iota(jnp.int32, (loc, loc), 1) // group
    same_group = jnp.where(chan_row == chan_col, 1.0, 0.0).astype(F32)
    lane = lax.broadcasted_iota(jnp.int32, (loc, cols), 1)

    def group_total(values):
        summed = jnp.sum(values, axis=1, keepdims=True)
        wide = jnp.broadcast_to(summed, (loc, cols))
        return jnp.dot(same_group, wide, precision=HIGH, preferred_element_type=F32)

    sums = [jnp.zeros((loc, cols), F32) for _ in range(4)]
    for j in range(slots):
        x0 = lat[j, 0].astype(F32)
        total, square = x0, x0 * x0
        for t in range(1, trows):
            xt = lat[j, t].astype(F32)
            total, square = total + xt, square + xt * xt
        sums = [
            sums[0] + mask_a[j] * total, sums[1] + mask_a[j] * square,
            sums[2] + mask_b[j] * total, sums[3] + mask_b[j] * square,
        ]
    for i, count in enumerate((count_a, count_b)):
        mean = group_total(sums[2 * i]) / count
        var = group_total(sums[2 * i + 1]) / count - mean * mean
        stat[i, 0] = mean
        stat[i, 1] = lax.rsqrt(var + EPS)

    def pre_of(r):
        j = r // trows
        mean, rstd = stat[is_b[j], 0], stat[is_b[j], 1]
        normed = (lat[j, r % trows].astype(F32) - mean) * rstd
        return normed, normed * gain + bias, rstd

    mine = pl.ds(pl.multiple_of(ch * loc, 16), loc)

    def ag_copy(kind, c):
        source = (mybuf.at[c], mybuf.at[c], agbuf.at[1, c])[kind]
        return rc(
            source, agbuf.at[kind, c], ag_send.at[kind, c], ag_recv.at[kind, c],
            chan=(sib, xn, sib)[kind],
        )

    pl.semaphore_wait(barrier, n + 1)
    for c in range(CHUNKS):
        for r in range(c * nrow // CHUNKS, (c + 1) * nrow // CHUNKS):
            _, pre, _ = pre_of(r)
            value = pre * jax.nn.sigmoid(pre) * used[r // trows]
            mybuf[c, :, pl.ds(r * cols - c * span, cols)] = value.astype(BF16)
        ag_copy(1, c).start()
        ag_copy(0, c).start()

    pad = padded - rows9
    full_blocks = rows9 // 128
    for i in range(full_blocks):
        w_t[:, pl.ds(i * 128, 128)] = w[pl.ds(i * 128, 128), :].T
    rest = rows9 - full_blocks * 128
    if rest:
        tail = jnp.concatenate(
            [w[pl.ds(full_blocks * 128, rest), :], jnp.zeros((128 - rest, chans), BF16)], axis=0
        )
        w_t[:, pl.ds(full_blocks * 128, 128)] = tail.T
        done = (full_blocks + 1) * 128
    else:
        done = rows9
    if done < rows9 + pad:
        w_t[:, pl.ds(done, rows9 + pad - done)] = jnp.zeros((chans, rows9 + pad - done), BF16)
    field[pl.ds(rows9, pad), :] = jnp.zeros((pad, nrow * cols), BF16)
    third = rows9 // 3
    field[pl.ds(0, third), pl.ds((nrow - 1) * cols, cols)] = jnp.zeros((third, cols), BF16)
    field[pl.ds(2 * third, third), pl.ds(0, cols)] = jnp.zeros((third, cols), BF16)

    def from_left(v):
        return jnp.where(lane == 0, 0.0, pltpu.roll(v, 1, 1))

    def from_right(v):
        return jnp.where(lane == cols - 1, 0.0, pltpu.roll(v, cols - 1, 1))

    def taps(row_tap, col_tap, r):
        return pre_w[pl.ds((row_tap * 3 + col_tap) * loc, loc), pl.ds(r * cols, cols)]

    def out_row(r):
        j = r // trows
        total = []
        for col_tap in range(3):
            value = taps(1, col_tap, r)
            if r > 0:
                value = value + up[r] * taps(0, col_tap, r - 1)
            if r < nrow - 1:
                value = value + down[r] * taps(2, col_tap, r + 1)
            total.append(value)
        pred = total[1] + from_left(total[0]) + from_right(total[2])
        grad = loss[j] * (pred - tgt[j, r % trows].astype(F32))
        grad = grad.astype(BF16).astype(F32)
        for col_tap, moved in enumerate((from_right(grad), grad, from_left(grad))):
            def put(row_tap, row, value):
                field[
                    pl.ds((row_tap * 3 + col_tap) * loc, loc), pl.ds(row * cols, cols)
                ] = value.astype(BF16)
            put(1, r, moved)
            if r > 0:
                put(0, r - 1, up[r] * moved)
            if r < nrow - 1:
                put(2, r + 1, down[r] * moved)

    rows_chunk = nrow // CHUNKS
    for c in range(CHUNKS):
        ag_copy(1, c).wait_recv()
        ag_copy(2, c).start()
        ag_copy(0, c).wait_recv()
        ag_copy(2, c).wait_recv()
        here = pl.ds(c * span, span)
        act[mine, here] = mybuf[c]
        for kind, index in enumerate((sib, xn, diag)):
            act[pl.ds(pl.multiple_of(index * loc, 16), loc), here] = agbuf[kind, c]
        for i in range(3):
            pre_w[pl.ds(i * third, third), here] = jnp.dot(
                w[pl.ds(i * third, third), :], act[:, here], preferred_element_type=F32
            )
        act_t[here, :] = act[:, here].T
        low = max(0, c * rows_chunk - 1)
        high = nrow if c == CHUNKS - 1 else (c + 1) * rows_chunk - 1
        for r in range(low, high):
            out_row(r)

    def weight_part(y):
        start = pl.multiple_of(y * half, 16)
        total = jnp.dot(field[pl.ds(start, half), :], act_t[...], preferred_element_type=F32)
        return (total * grad_scale).astype(BF16).reshape(nz, piece, chans)

    def y_copy(k):
        return rc(
            wy.at[lax.rem(my_z + k, nz)], ybuf.at[k], y_send.at[k], y_recv.at[k], space=y_dev
        )

    order = list(range(1, nz)) + [0]
    wy[...] = weight_part(1 - my_y)
    for k in order:
        y_copy(k).start()
    wbuf[...] = weight_part(my_y)

    for c in range(CHUNKS):
        here = pl.ds(c * span, span)
        part[:, here] = jnp.dot(
            w_t[...], field[:, here], preferred_element_type=F32
        ).astype(BF16)

    def block(index):
        return pl.ds(pl.multiple_of(index * loc, 16), loc)

    far_copy = rc(part.at[block(diag)], sib_far, r_send.at[0], r_recv.at[0], chan=sib)
    near_copy = rc(part.at[block(sib)], sib_near, r_send.at[1], r_recv.at[1], chan=sib)
    x_copy = rc(x_send, x_recv, r_send.at[2], r_recv.at[2], chan=xn)
    far_copy.start()
    near_copy.start()
    far_copy.wait_recv()
    x_send[...] = (part[block(xn), :].astype(F32) + sib_far[...].astype(F32)).astype(BF16)
    x_copy.start()

    def z_copy(k):
        z = lax.rem(my_z + k, nz)
        return rc(
            zsend.at[k], zbuf.at[k], z_send.at[k], z_recv.at[k], space=z * 2 + my_y
        )

    for k in order:
        y_copy(k).wait_recv()
        z = lax.rem(my_z + k, nz)
        zsend[k] = (wbuf[z].astype(F32) + ybuf[k].astype(F32)).astype(BF16)
        if k:
            z_copy(k).start()

    near_copy.wait_recv()
    x_copy.wait_recv()
    sums = [jnp.zeros((loc, cols), F32) for _ in range(4)]
    for j in range(slots):
        total, second = None, None
        for t in range(trows):
            r = j * trows + t
            at = pl.ds(r * cols, cols)
            grad = (
                part[mine, at].astype(F32) + sib_near[:, at].astype(F32)
            ) + x_recv[:, at].astype(F32)
            normed, pre, _ = pre_of(r)
            s = jax.nn.sigmoid(pre)
            value = grad * (s * (1.0 + pre * (1.0 - s))) * gain
            ngrad[r] = value
            total = value if total is None else total + value
            second = value * normed if second is None else second + value * normed
        sums = [
            sums[0] + mask_a[j] * total, sums[1] + mask_a[j] * second,
            sums[2] + mask_b[j] * total, sums[3] + mask_b[j] * second,
        ]
    for i, count in enumerate((count_a, count_b)):
        stat[i, 2] = group_total(sums[2 * i]) / count
        stat[i, 3] = group_total(sums[2 * i + 1]) / count
    for r in range(nrow):
        j = r // trows
        normed, _, rstd = pre_of(r)
        mean_g, mean_gn = stat[is_b[j], 2], stat[is_b[j], 3]
        xg[j, r % trows] = (rstd * (ngrad[r] - mean_g - normed * mean_gn)).astype(BF16)
    for k in range(n):
        d = lax.rem(me + k, n)
        slot = jnp.int32(0)
        for j in range(slots):
            slot = jnp.where(to[me, j] == d, j, slot)
        if k:
            outg[k] = xg[slot]
        else:
            inb[0] = xg[slot]

    def a_copy(k):
        return rc(
            outg.at[k], inb.at[k], a_send.at[k], a_recv.at[k], space=lax.rem(me + k, n)
        )

    for k in range(1, n):
        a_copy(k).start()

    total = zsend[0].astype(F32)
    for k in range(1, nz):
        z_copy(k).wait_recv()
        total = total + zbuf[k].astype(F32)
    own[...] = total.astype(BF16)

    def gz_copy(k):
        z = lax.rem(my_z + k, nz)
        return rc(own, gzbuf.at[k], gz_send.at[k], gz_recv.at[k], space=z * 2 + my_y)

    def gy_copy(k):
        source = gzbuf.at[k] if k else own
        return rc(source, gybuf.at[k], gy_send.at[k], gy_recv.at[k], space=y_dev)

    for k in range(1, nz):
        gz_copy(k).start()
    gy_copy(0).start()

    def put_piece(y, k, value):
        z = lax.rem(my_z - k + nz, nz)
        res[pl.ds(pl.multiple_of((y * nz + z) * piece, 16), piece), :] = value

    put_piece(my_y, 0, own[...])
    for k in range(1, nz):
        gz_copy(k).wait_recv()
        gy_copy(k).start()
        put_piece(my_y, k, gzbuf[k])

    def find(step, found):
        s, j = step // slots, lax.rem(step, slots)
        owner, place = to[s, j], ts[s, j]
        return tuple(
            jnp.where((owner == me) & (place == t), s, found[t]) for t in range(tiles_dev)
        )

    found = lax.fori_loop(0, n * slots, find, tuple(jnp.int32(0) for _ in range(tiles_dev)))
    for k in range(1, n):
        a_copy(k).wait_recv()
    for t in range(tiles_dev):
        xo[t] = inb[lax.rem(me - found[t] + n, n)]
    for k in range(nz):
        gy_copy(k).wait_recv()
        put_piece(1 - my_y, k, gybuf[k])
    wo[...] = res[pl.ds(0, rows9), :]

    for c in range(CHUNKS):
        for kind in range(3):
            ag_copy(kind, c).wait_send()
    for z in range(nz):
        y_copy(z).wait_send()
        gy_copy(z).wait_send()
    for k in range(1, nz):
        z_copy(k).wait_send()
        gz_copy(k).wait_send()
    for k in range(1, n):
        a_copy(k).wait_send()
    for copy in (far_copy, near_copy, x_copy):
        copy.wait_send()


def local(
    latents, targets, norm_gain, norm_bias, conv_weight, tile_image, tile_owner, tile_slot,
    timesteps,
):
    n = lax.axis_size("space")
    slots, trows, loc, cols = latents.shape
    chans = conv_weight.shape[3]
    tiles_dev = slots // 2
    rows9 = 9 * loc
    wide = slots * trows * cols
    step = math.lcm(16 * n, 256)
    padded = -(-rows9 // step) * step
    nz = n // 2
    piece = padded // n
    grad_scale = 1.0 / math.sqrt(n * tiles_dev * trows * cols)
    gb = jnp.broadcast_to(
        jnp.stack([norm_gain, norm_bias])[:, :, None], (2, loc, cols)
    )
    smem = pl.BlockSpec(memory_space=pltpu.SMEM)
    vmem = pl.BlockSpec(memory_space=pltpu.VMEM)
    dma = pltpu.SemaphoreType.DMA
    x_grad, weight = pl.pallas_call(
        functools.partial(kernel, n, grad_scale),
        out_shape=(
            jax.ShapeDtypeStruct((tiles_dev, trows, loc, cols), BF16),
            jax.ShapeDtypeStruct((rows9, chans), BF16),
        ),
        in_specs=[smem] * 4 + [vmem] * 4,
        out_specs=(vmem, vmem),
        scratch_shapes=[
            pltpu.VMEM((chans, wide), BF16),
            pltpu.VMEM((CHUNKS, loc, wide // CHUNKS), BF16),
            pltpu.VMEM((3, CHUNKS, loc, wide // CHUNKS), BF16),
            pltpu.VMEM((wide, chans), BF16),
            pltpu.VMEM((rows9, wide), F32),
            pltpu.VMEM((padded, wide), BF16),
            pltpu.VMEM((chans, padded), BF16),
            *[pltpu.VMEM((nz, piece, chans), BF16)] * 5,
            pltpu.VMEM((piece, chans), BF16),
            *[pltpu.VMEM((nz, piece, chans), BF16)] * 2,
            pltpu.VMEM((padded, chans), BF16),
            pltpu.VMEM((chans, wide), BF16),
            pltpu.VMEM((loc, wide), BF16),
            pltpu.VMEM((loc, wide), BF16),
            pltpu.VMEM((loc, wide), BF16),
            pltpu.VMEM((loc, wide), BF16),
            pltpu.VMEM((2, 4, loc, cols), F32),
            pltpu.VMEM((slots * trows, loc, cols), F32),
            pltpu.VMEM((slots, trows, loc, cols), BF16),
            pltpu.VMEM((n, trows, loc, cols), BF16),
            pltpu.VMEM((n, trows, loc, cols), BF16),
            dma((3, CHUNKS)), dma((3, CHUNKS)),
            dma((nz,)), dma((nz,)), dma((nz,)), dma((nz,)), dma((nz,)), dma((nz,)),
            dma((nz,)), dma((nz,)), dma((n,)), dma((n,)), dma((3,)), dma((3,)),
        ],
        compiler_params=pltpu.CompilerParams(
            collective_id=0, has_side_effects=True, vmem_limit_bytes=62 * 1024 * 1024
        ),
    )(
        tile_image, tile_owner, tile_slot, loss_weights(timesteps), gb, latents, targets,
        conv_weight.reshape(rows9, chans),
    )
    return x_grad, weight.astype(F32).reshape(conv_weight.shape)


def solution(mesh):
    in_specs = (
        P("space", None, "chan", None),
        P("space", None, "chan", None),
        P("chan"),
        P("chan"),
        P(None, None, "chan", None),
        P(),
        P(),
        P(),
        P(),
    )
    out_specs = (P("space", None, "chan", None), P(None, None, "chan", None))
    return jax.shard_map(local, mesh=mesh, in_specs=in_specs, out_specs=out_specs, check_vma=False)
```
